32 devices in a mesh: section: 2 (over x), tensor: 4 (over y, core), dp: 4 (over z).
Axes of the slice: x: 2, y: 2, z: 4, core: 2. Of those that a mesh axis runs over, the one named last changes fastest.
Arguments:
- target_ids: int32 [4, 512], P(None, 'section'), may hold values from 0 to 32127
- embed_table: bfloat16 [32128, 4096], P('dp', 'tensor'), may hold values from -16 to 16
- encoder_out: bfloat16 [4, 512, 4096], P('dp', 'section', 'tensor'), may hold values from -32 to 32
- w_query: bfloat16 [4096, 4096], P(('section', 'dp'), 'tensor'), may hold values from -1 to 1
- w_key: bfloat16 [4096, 4096], P(('section', 'dp'), 'tensor'), may hold values from -1 to 1
- w_value: bfloat16 [4096, 4096], P(('section', 'dp'), 'tensor'), may hold values from -0.09375 to 0.09375
Outputs:
- attended: bfloat16 [4, 512, 4096], P('dp', 'section', 'tensor')
The draws below stay inside these ranges and needn't reach their ends.
All inputs are finite; a program needn't handle non-finite values.
Results may differ from the reference program's by a relative error of at most 0.0096.
Values may be sent and summed in bfloat16 or wider, within the bound.
A program may use at most 128 MiB of HBM per device.

```python
import math
import jax
import jax.numpy as jnp
from jax import lax

D = 4096
HEADS = 16
HD = 256
V = 32128
L = 512
BATCH = 4


def query_matrix(key):
    normal_part = jnp.clip(jax.random.normal(jax.random.fold_in(key, 11), (D, HEADS * HD), jnp.float32), -6.0, 6.0)
    return 1.6 * normal_part / math.sqrt(D)


def draw_w_query(key, part):
    return jnp.clip(query_matrix(key), -1.0, 1.0).astype(jnp.bfloat16)


def draw_w_key(key, part):
    normal_part = jnp.clip(jax.random.normal(jax.random.fold_in(key, 12), (D, HEADS * HD), jnp.float32), -6.0, 6.0)
    other = 1.6 * normal_part / math.sqrt(D)
    result = other
    return jnp.clip(result, -1.0, 1.0).astype(jnp.bfloat16)


def draw_embed_table(key, part):
    normal_part = jnp.clip(jax.random.normal(jax.random.fold_in(key, 1), (V, D), jnp.float32), -6.0, 6.0)
    result = normal_part
    return jnp.clip(result, -16.0, 16.0).astype(jnp.bfloat16)


def draw_encoder_out(key, part):
    normal_part = jnp.clip(jax.random.normal(jax.random.fold_in(key, 3), (BATCH, L, D), jnp.float32), -6.0, 6.0)
    result = normal_part
    return jnp.clip(result, -32.0, 32.0).astype(jnp.bfloat16)


def touch_ends(entries, own_key, smallest, high):
    index_at = [jax.random.randint(jax.random.fold_in(own_key, axis), (), 0, length) for axis, length in enumerate(entries.shape)]
    widest = entries.shape.index(max(entries.shape))
    next_to = index_at[:widest] + [(index_at[widest] + 1) % entries.shape[widest]] + index_at[widest + 1:]
    return entries.at[tuple(index_at)].set(smallest).at[tuple(next_to)].set(high)


def steps_of(own_key, shape, cuts, low, largest):
    def one(position, blocks):
        draws = jax.random.uniform(jax.random.fold_in(jax.random.fold_in(own_key, 6), position), (blocks,), jnp.float32, low / len(cuts), largest / len(cuts))
        return jnp.repeat(jnp.exp(draws), shape[position] // blocks).reshape((-1,) + (1,) * (len(shape) - position - 1))

    gain = one(*cuts[0])
    for cut in cuts[1:]:
        gain = gain * one(*cut)
    return gain


def centred(stream_key, shape, deviation, limit, pieces=(), kind=jnp.bfloat16):
    factor_of = steps_of(stream_key, shape, pieces, -0.22, 0.18) if pieces else 1.0
    array = jax.random.normal(stream_key, shape, jnp.float32) * deviation * factor_of
    return jnp.minimum(jnp.maximum(array, -limit), limit).astype(kind)


def setup_inputs(seed: int = 0) -> dict:
    splits = jax.random.split(jax.random.key(seed), 7)
    return {
        "target_ids": touch_ends(jax.random.randint(splits[0], (BATCH, L), 0, V), jax.random.fold_in(splits[0], 1), 0, V - 1).astype(jnp.int32),
        "embed_table": draw_embed_table(jax.random.fold_in(splits[6], 71), 0),
        "encoder_out": draw_encoder_out(jax.random.fold_in(splits[6], 71), 0),
        "w_query": draw_w_query(jax.random.fold_in(splits[6], 71), 0),
        "w_key": draw_w_key(jax.random.fold_in(splits[6], 71), 0),
        "w_value": centred(splits[5], (D, HEADS * HD), D ** -0.5, 0.09375, ((0, 8), (1, 4))),
    }


def reference(target_ids, embed_table, encoder_out, w_query, w_key, w_value):
    decoder_in = jnp.take(embed_table, target_ids, axis=0)
    queries = jnp.dot(decoder_in.reshape(-1, D), w_query, preferred_element_type=jnp.float32).astype(jnp.bfloat16)
    memory = encoder_out.reshape(-1, D)
    keys = jnp.dot(memory, w_key, preferred_element_type=jnp.float32).astype(jnp.bfloat16)
    values = jnp.dot(memory, w_value, preferred_element_type=jnp.float32).astype(jnp.bfloat16)
    queries = queries.reshape(BATCH, L, HEADS, HD)
    keys = keys.reshape(BATCH, L, HEADS, HD)
    values = values.reshape(BATCH, L, HEADS, HD)
    logit_scale_factor = HD ** -0.5

    def one_head(head_index):
        head_query_slice = lax.dynamic_index_in_dim(queries, head_index, 2, keepdims=False).astype(jnp.float32)
        head_key_slice = lax.dynamic_index_in_dim(keys, head_index, 2, keepdims=False).astype(jnp.float32)
        head_value_slice = lax.dynamic_index_in_dim(values, head_index, 2, keepdims=False).astype(jnp.float32)
        attention_logits = jnp.einsum("trw,tew->tre", head_query_slice, head_key_slice) * logit_scale_factor
        peaks = jnp.max(attention_logits, axis=-1, keepdims=True)
        weights = jnp.exp(attention_logits - peaks)
        weight_sum = jnp.sum(weights, axis=-1, keepdims=True)
        reduced_precision_weights = lax.optimization_barrier(weights.astype(jnp.bfloat16)).astype(jnp.float32)
        weighted_value_total = jnp.einsum("onh,ohf->onf", reduced_precision_weights, head_value_slice, precision=lax.Precision.HIGHEST)
        return (weighted_value_total / weight_sum).astype(jnp.bfloat16)

    heads_out = lax.map(one_head, jnp.arange(HEADS, dtype=jnp.int32))
    return jnp.transpose(heads_out, (1, 2, 0, 3)).reshape(BATCH, L, HEADS * HD)
```

```python
import jax
import jax.numpy as jnp
from jax import lax
from jax.sharding import PartitionSpec as P

HD = 256


def contract(segment, weight):
    return jnp.dot(segment, weight, preferred_element_type=jnp.float32)


def make(mesh):
    sections, tensors, planes = (mesh.shape[a] for a in ("section", "tensor", "dp"))

    def to_planes(rows):
        positions = rows.shape[0]
        mine = lax.all_to_all(rows, "tensor", split_axis=0, concat_axis=1, tiled=True)
        depth = mine.shape[1] // (sections * planes)
        mine = mine.reshape(positions // tensors, sections, planes, depth)
        mine = jnp.transpose(mine, (2, 0, 1, 3)).reshape(planes, positions // tensors, sections * depth)
        mine = lax.all_to_all(mine, "dp", split_axis=0, concat_axis=0, tiled=True)
        return lax.all_gather(mine, "tensor", axis=1, tiled=True)

    def project(sources, weights):
        plane = lax.axis_index("dp")

        def partial(index):
            index = jnp.clip(index, 0, planes - 1)
            block = lax.dynamic_index_in_dim(sources, index, 0, keepdims=False)
            return [contract(block, weight) for weight in weights]

        above = below = None
        for step in range(planes - 1):
            away = planes - 1 - step
            up, down = partial(plane + away), partial(plane - away)
            if above is not None:
                up = [a + b for a, b in zip(up, below)]
                down = [a + b for a, b in zip(down, above)]
            up_pairs = [(i, i + 1) for i in range(step + 1)]
            down_pairs = [(planes - 1 - i, planes - 2 - i) for i in range(step + 1)]
            below = [lax.ppermute(a.astype(jnp.bfloat16), "dp", up_pairs).astype(jnp.float32) for a in up]
            above = [lax.ppermute(a.astype(jnp.bfloat16), "dp", down_pairs).astype(jnp.float32) for a in down]
        own = partial(plane)
        if above is not None:
            own = [a + b + c for a, b, c in zip(own, above, below)]
        return [a.astype(jnp.bfloat16) for a in own]

    def on_device(target_ids, embed_table, encoder_out, w_query, w_key, w_value):
        table_rows = embed_table.shape[0]
        offset_ids = target_ids - lax.axis_index("dp") * table_rows
        inside = (offset_ids >= 0) & (offset_ids < table_rows)
        picked = jnp.take(embed_table, jnp.clip(offset_ids, 0, table_rows - 1), axis=0)
        picked = jnp.where(inside[..., None], picked, jnp.zeros((), picked.dtype))
        key_weight, value_weight, query_weight = (
            lax.all_gather(w, "section", axis=0, tiled=True) for w in (w_key, w_value, w_query)
        )
        memory = to_planes(encoder_out[0])
        keys_local, values_local = project(memory, (key_weight, value_weight))
        key_rows = lax.all_gather(keys_local, "section", axis=0, tiled=True)
        value_rows = lax.all_gather(values_local, "section", axis=0, tiled=True)
        decoder_in = lax.psum_scatter(picked, "dp", scatter_dimension=0, tiled=True)
        (queries,) = project(to_planes(decoder_in[0]), (query_weight,))
        positions, columns = queries.shape
        heads_here = columns // HD
        query_heads = queries.reshape(positions, heads_here, HD)
        key_block = key_rows.reshape(-1, heads_here, HD)
        value_block = value_rows.reshape(-1, heads_here, HD)
        scores = (
            jnp.einsum("phd,nhd->hpn", query_heads, key_block, preferred_element_type=jnp.float32)
            * HD ** (-0.5)
        )
        weights = jnp.exp(scores - jnp.max(scores, axis=-1, keepdims=True))
        weight_sum = jnp.sum(weights, axis=-1)
        total = jnp.einsum(
            "hpn,nhd->hpd", weights.astype(jnp.bfloat16), value_block, preferred_element_type=jnp.float32
        )
        result = jnp.transpose(total / weight_sum[..., None], (1, 0, 2))
        return result.reshape(positions, columns).astype(jnp.bfloat16)[None]

    return on_device


def solution(mesh):
    in_specs = (
        P(None, "section"),
        P("dp", "tensor"),
        P("dp", "section", "tensor"),
        P(("section", "dp"), "tensor"),
        P(("section", "dp"), "tensor"),
        P(("section", "dp"), "tensor"),
    )
    out_specs = P("dp", "section", "tensor")
    return jax.shard_map(
        make(mesh), mesh=mesh, in_specs=in_specs, out_specs=out_specs, check_vma=False
    )
```

```python
import functools

import jax
import jax.numpy as jnp
from jax import lax
from jax.experimental import pallas as pl
from jax.experimental.pallas import tpu as pltpu
from jax.sharding import PartitionSpec as P

HD = 256
KEY, VALUE, QUERY = 0, 1, 2
ENCODER, DECODER = 0, 1


def project_kernel(
    sections, tensors, planes,
    enc, picks, w_key, w_value, w_query,
    q_out, k_out, v_out,
    wbuf, x_enc, x_dec, rs_up, rs_dn, rs_out, sums, up, dn,
    w_local, w_send, w_recv, z_send, z_recv, e_send, e_recv,
    r_send, r_up, r_dn, c_send, c_up, c_dn, o_send, o_recv,
):
    s, t, d = lax.axis_index("section"), lax.axis_index("tensor"), lax.axis_index("dp")
    depth, columns = w_key.shape
    blocks = enc.shape[1] // depth
    groups = planes // blocks
    rank, group = t // groups, lax.rem(t, groups)
    owner = group == d // blocks
    tile = min(columns, 256)
    sent = []

    def remote(src, dst, send_sem, recv_sem, **device):
        return pltpu.make_async_remote_copy(
            src_ref=src, dst_ref=dst, send_sem=send_sem, recv_sem=recv_sem,
            device_id=device, device_id_type=pl.DeviceIdType.MESH,
        )

    def send(when, src, dst, send_sem, recv_sem, **device):
        copy = remote(src, dst, send_sem, recv_sem, **device)
        sent.append((when, copy))

        @pl.when(when)
        def _():
            copy.start()

    def received(dst, recv_sem):
        remote(dst, dst, c_send.at[0, 0], recv_sem, dp=lax.rem(d + 1, planes)).wait_recv()

    always = d >= 0
    barrier = pltpu.get_barrier_semaphore()
    for axis, index, size in (("section", s, sections), ("tensor", t, tensors), ("dp", d, planes)):
        for shift in range(1, size):
            pl.semaphore_signal(
                barrier, inc=1, device_id={axis: lax.rem(index + shift, size)},
                device_id_type=pl.DeviceIdType.MESH,
            )
    pl.semaphore_wait(barrier, sections + tensors + planes - 3)

    def start_weight(j, weight):
        for shift in range(1, sections):
            send(always, weight, wbuf.at[j, s], w_send.at[j, shift], w_recv.at[j, s],
                 section=lax.rem(s + shift, sections))

    def have_weight(j):
        for shift in range(1, sections):
            other = lax.rem(s + shift, sections)
            received(wbuf.at[j, other], w_recv.at[j, other])

    def part(ref, i):
        return ref.at[:, pl.ds(i * depth, depth)]

    for i in range(blocks):
        plane = group * blocks + i
        send(plane != d, part(enc, i), x_enc.at[d, rank], z_send.at[i], z_recv.at[d], dp=plane)
    start_weight(KEY, w_key)
    for i in range(blocks):
        plane = group * blocks + i
        src = picks.at[:, :, pl.ds(i * depth, depth)]
        rising, falling = (d == 0) & (plane > d), (d == planes - 1) & (plane < d)
        send(rising, src, rs_up.at[i], r_send.at[i], r_up.at[i], dp=lax.rem(d + 1, planes))
        send(falling, src, rs_dn.at[i], r_send.at[i], r_dn.at[i], dp=lax.rem(d + planes - 1, planes))
    local = [
        pltpu.make_async_copy(w, wbuf.at[j, s], w_local.at[j])
        for j, w in enumerate((w_key, w_value, w_query))
    ]
    for copy in local:
        copy.start()
    for i in range(blocks):

        @pl.when(group * blocks + i == d)
        def _():
            x_enc[d, rank] = enc[:, pl.ds(i * depth, depth)]

    def clear(ref):
        @pl.loop(0, 3 * planes)
        def _(n):
            ref[n // planes, lax.rem(n, planes)] = jnp.zeros(ref.shape[2:], ref.dtype)

    pl.when(d == 0)(lambda: clear(up))
    pl.when(d == planes - 1)(lambda: clear(dn))

    def spread(kind, buffer):
        for b in sorted(range(planes), key=lambda b: (min(b, planes - 1 - b), -b)):
            if kind == ENCODER:

                @pl.when(owner & (d != b))
                def _():
                    received(buffer.at[b, rank], z_recv.at[b])

            for shift in range(1, tensors):
                send(owner, buffer.at[b, rank], buffer.at[b, rank], e_send.at[kind, b, shift],
                     e_recv.at[kind, b, rank], tensor=lax.rem(t + shift, tensors))

    def have_spread(kind, buffer, b):
        for k in range(sections):

            @pl.when(k * groups + d // blocks != t)
            def _():
                received(buffer.at[b, k], e_recv.at[kind, b, k])

    def forward_rows(stage):
        for i in range(blocks):
            plane = group * blocks + i
            rising, falling = (d == stage) & (plane > d), (d == planes - 1 - stage) & (plane < d)
            for moving, held, sem, to in ((rising, rs_up, r_up, 1), (falling, rs_dn, r_dn, planes - 1)):

                @pl.when(moving)
                def _():
                    received(held.at[i], sem.at[i])

                    @pl.loop(0, planes)
                    def _(b):
                        rs_out[i, b] = picks[b, :, pl.ds(i * depth, depth)] + held[i, b]

                send(moving, rs_out.at[i], held.at[i], r_send.at[i], sem.at[i], dp=lax.rem(d + to, planes))

    def finish_rows():
        for i in range(blocks):
            mine = group * blocks + i == d

            @pl.when(mine)
            def _():
                @pl.loop(0, planes)
                def _(b):
                    x_dec[b, rank] = picks[b, :, pl.ds(i * depth, depth)]

            for has, held, sem in ((d > 0, rs_up, r_up), (d < planes - 1, rs_dn, r_dn)):

                @pl.when(mine & has)
                def _():
                    received(held.at[i], sem.at[i])

                    @pl.loop(0, planes)
                    def _(b):
                        x_dec[b, rank] = x_dec[b, rank] + held[i, b]

    def product(j, x, b, cols):
        total = None
        for k in range(sections):
            term = jnp.dot(x[b, k], wbuf[j, k, :, cols], preferred_element_type=jnp.float32)
            total = term if total is None else total + term
        return total

    def chain(j, x):
        for step in range(planes - 1):
            for b, to, held, sem, has in (
                (planes - 1 - step, 1, up, c_up, d > 0),
                (step, planes - 1, dn, c_dn, d < planes - 1),
            ):
                moving = b > d if to == 1 else b < d

                @pl.when(moving)
                def _():
                    @pl.when(has)
                    def _():
                        received(held.at[j, b], sem.at[j, b])

                    @pl.loop(0, columns // tile)
                    def _(n):
                        cols = pl.ds(pl.multiple_of(n * tile, tile), tile)
                        total = product(j, x, b, cols) + held[j, b, :, cols].astype(jnp.float32)
                        sums[j, b, :, cols] = total.astype(jnp.bfloat16)

                send(moving, sums.at[j, b], held.at[j, b], c_send.at[j, b], sem.at[j, b],
                     dp=lax.rem(d + to, planes))

    def finish(j, x, out):
        @pl.when(d > 0)
        def _():
            received(up.at[j, d], c_up.at[j, d])

        @pl.when(d < planes - 1)
        def _():
            received(dn.at[j, d], c_dn.at[j, d])

        @pl.loop(0, columns // tile)
        def _(n):
            cols = pl.ds(pl.multiple_of(n * tile, tile), tile)
            arrived = up[j, d, :, cols].astype(jnp.float32) + dn[j, d, :, cols].astype(jnp.float32)
            out[:, cols] = (product(j, x, d, cols) + arrived).astype(jnp.bfloat16)

    def share(j, out):
        for shift in range(1, sections):
            send(always, out.at[s], out.at[s], o_send.at[j, shift], o_recv.at[j, s],
                 section=lax.rem(s + shift, sections))

    spread(ENCODER, x_enc)
    forward_rows(1)
    for copy in local:
        copy.wait()
    for b in range(planes):
        have_spread(ENCODER, x_enc, b)
    have_weight(KEY)
    start_weight(VALUE, w_value)
    chain(KEY, x_enc)
    for stage in range(2, planes - 1):
        forward_rows(stage)
    have_weight(VALUE)
    start_weight(QUERY, w_query)
    chain(VALUE, x_enc)
    finish_rows()
    spread(DECODER, x_dec)
    finish(KEY, x_enc, k_out.at[s])
    have_weight(QUERY)
    share(KEY, k_out)
    for b in range(planes):
        have_spread(DECODER, x_dec, b)
    chain(QUERY, x_dec)
    finish(VALUE, x_enc, v_out.at[s])
    share(VALUE, v_out)
    finish(QUERY, x_dec, q_out)
    for j, out in ((KEY, k_out), (VALUE, v_out)):
        for shift in range(1, sections):
            other = lax.rem(s + shift, sections)
            received(out.at[other], o_recv.at[j, other])
    for when, copy in sent:
        pl.when(when)(copy.wait_send)


def projections(mesh, enc, picks, w_key, w_value, w_query):
    sections, tensors, planes = (mesh.shape[a] for a in ("section", "tensor", "dp"))
    positions = enc.shape[0]
    depth, columns = w_key.shape
    blocks = enc.shape[1] // depth
    bf16 = jnp.bfloat16
    dma = pltpu.SemaphoreType.DMA
    rows = (planes, sections, positions, depth)
    moving = (blocks, planes, positions, depth)
    chains = (3, planes, positions, columns)
    vmem = pl.BlockSpec(memory_space=pltpu.VMEM)
    hbm = pl.BlockSpec(memory_space=pl.ANY)
    return pl.pallas_call(
        functools.partial(project_kernel, sections, tensors, planes),
        out_shape=(
            jax.ShapeDtypeStruct((positions, columns), bf16),
            jax.ShapeDtypeStruct((sections, positions, columns), bf16),
            jax.ShapeDtypeStruct((sections, positions, columns), bf16),
        ),
        in_specs=[vmem, vmem, hbm, hbm, hbm],
        out_specs=(vmem, vmem, vmem),
        scratch_shapes=[
            pltpu.VMEM((3, sections, depth, columns), bf16),
            pltpu.VMEM(rows, bf16),
            pltpu.VMEM(rows, bf16),
            pltpu.VMEM(moving, bf16),
            pltpu.VMEM(moving, bf16),
            pltpu.VMEM(moving, bf16),
            pltpu.VMEM(chains, bf16),
            pltpu.VMEM(chains, bf16),
            pltpu.VMEM(chains, bf16),
            dma((3,)),
            dma((3, sections)),
            dma((3, sections)),
            dma((blocks,)),
            dma((planes,)),
            dma((2, planes, tensors)),
            dma((2, planes, sections)),
            dma((blocks,)),
            dma((blocks,)),
            dma((blocks,)),
            dma((3, planes)),
            dma((3, planes)),
            dma((3, planes)),
            dma((2, sections)),
            dma((2, sections)),
        ],
        compiler_params=pltpu.CompilerParams(
            collective_id=0, has_side_effects=True, vmem_limit_bytes=56 * 2**20
        ),
        cost_estimate=pl.CostEstimate(
            flops=6 * planes * positions * sections * depth * columns,
            bytes_accessed=2 * (picks.size + 3 * w_key.size),
            transcendentals=0,
        ),
    )(enc, picks, w_key, w_value, w_query)


def make(mesh):
    def on_device(target_ids, embed_table, encoder_out, w_query, w_key, w_value):
        table_rows = embed_table.shape[0]
        offset_ids = target_ids - lax.axis_index("dp") * table_rows
        inside = (offset_ids >= 0) & (offset_ids < table_rows)
        picked = jnp.take(embed_table, jnp.clip(offset_ids, 0, table_rows - 1), axis=0)
        picked = jnp.where(inside[..., None], picked, jnp.zeros((), picked.dtype))
        queries, key_rows, value_rows = projections(mesh, encoder_out[0], picked, w_key, w_value, w_query)
        positions, columns = queries.shape
        heads_here = columns // HD
        query_heads = queries.reshape(positions, heads_here, HD)
        key_block = key_rows.reshape(-1, heads_here, HD)
        value_block = value_rows.reshape(-1, heads_here, HD)
        scores = (
            jnp.einsum("phd,nhd->hpn", query_heads, key_block, preferred_element_type=jnp.float32)
            * HD ** (-0.5)
        )
        weights = jnp.exp(scores - jnp.max(scores, axis=-1, keepdims=True))
        weight_sum = jnp.sum(weights, axis=-1)
        total = jnp.einsum(
            "hpn,nhd->hpd", weights.astype(jnp.bfloat16), value_block, preferred_element_type=jnp.float32
        )
        result = jnp.transpose(total / weight_sum[..., None], (1, 0, 2))
        return result.reshape(positions, columns).astype(jnp.bfloat16)[None]

    return on_device


def solution(mesh):
    in_specs = (
        P(None, "section"),
        P("dp", "tensor"),
        P("dp", "section", "tensor"),
        P(("section", "dp"), "tensor"),
        P(("section", "dp"), "tensor"),
        P(("section", "dp"), "tensor"),
    )
    out_specs = P("dp", "section", "tensor")
    return jax.shard_map(
        make(mesh), mesh=mesh, in_specs=in_specs, out_specs=out_specs, check_vma=False
    )
```

```python
import functools

import jax
import jax.numpy as jnp
from jax import lax
from jax.experimental import pallas as pl
from jax.experimental.pallas import tpu as pltpu
from jax.sharding import PartitionSpec as P

HD = 256
KEY, VALUE, QUERY = 0, 1, 2
ENCODER, DECODER = 0, 1


def project_kernel(
    sections, tensors, planes,
    enc, picks, w_key, w_value, w_query,
    out,
    k_all, v_all, wbuf, x_enc, x_dec, rs_up, rs_dn, rs_out, sums, up, dn,
    w_local, w_send, w_recv, z_send, z_recv, e_send, e_recv,
    r_send, r_up, r_dn, c_send, c_up, c_dn, o_send, o_recv,
):
    s, t, d = lax.axis_index("section"), lax.axis_index("tensor"), lax.axis_index("dp")
    depth, columns = w_key.shape
    blocks = enc.shape[1] // depth
    groups = planes // blocks
    rank, group = t // groups, lax.rem(t, groups)
    owner = group == d // blocks
    chunks = columns // HD
    edge = (d == 0) | (d == planes - 1)
    sent = []

    def remote(src, dst, send_sem, recv_sem, **device):
        return pltpu.make_async_remote_copy(
            src_ref=src, dst_ref=dst, send_sem=send_sem, recv_sem=recv_sem,
            device_id=device, device_id_type=pl.DeviceIdType.MESH,
        )

    def send(when, src, dst, send_sem, recv_sem, **device):
        copy = remote(src, dst, send_sem, recv_sem, **device)
        sent.append((when, copy))

        @pl.when(when)
        def _():
            copy.start()

    def received(dst, recv_sem):
        remote(dst, dst, c_send.at[0, 0, 0], recv_sem, dp=lax.rem(d + 1, planes)).wait_recv()

    always = d >= 0
    barrier = pltpu.get_barrier_semaphore()
    for axis, index, size in (("section", s, sections), ("tensor", t, tensors), ("dp", d, planes)):
        for shift in range(1, size):
            pl.semaphore_signal(
                barrier, inc=1, device_id={axis: lax.rem(index + shift, size)},
                device_id_type=pl.DeviceIdType.MESH,
            )
    pl.semaphore_wait(barrier, sections + tensors + planes - 3)

    def start_weight(j, weight):
        for shift in range(1, sections):
            send(always, weight, wbuf.at[j, s], w_send.at[j, shift], w_recv.at[j, s],
                 section=lax.rem(s + shift, sections))

    def have_weight(j):
        for shift in range(1, sections):
            other = lax.rem(s + shift, sections)
            received(wbuf.at[j, other], w_recv.at[j, other])

    def part(ref, i):
        return ref.at[:, pl.ds(i * depth, depth)]

    for i in range(blocks):
        plane = group * blocks + i
        send(plane != d, part(enc, i), x_enc.at[d, rank], z_send.at[i], z_recv.at[d], dp=plane)
    start_weight(KEY, w_key)
    for order, held, sem, end, to in (
        (reversed(range(blocks)), rs_up, r_up, 0, 1),
        (range(blocks), rs_dn, r_dn, planes - 1, planes - 1),
    ):
        for i in order:
            plane = group * blocks + i
            moving = (d == end) & ((plane > d) if to == 1 else (plane < d))
            for b in range(planes):
                src = picks.at[b, :, pl.ds(i * depth, depth)]
                send(moving, src, held.at[i, b], r_send.at[i, b], sem.at[i, b], dp=lax.rem(d + to, planes))
    local = [
        pltpu.make_async_copy(w, wbuf.at[j, s], w_local.at[j])
        for j, w in enumerate((w_key, w_value, w_query))
    ]
    for copy in local:
        copy.start()
    for i in range(blocks):

        @pl.when(group * blocks + i == d)
        def _():
            x_enc[d, rank] = enc[:, pl.ds(i * depth, depth)]

    def clear(ref):
        @pl.loop(0, 3 * planes)
        def _(n):
            ref[n // planes, lax.rem(n, planes)] = jnp.zeros(ref.shape[2:], ref.dtype)

    pl.when(d == 0)(lambda: clear(up))
    pl.when(d == planes - 1)(lambda: clear(dn))

    def spread(kind, buffer):
        for b in sorted(range(planes), key=lambda b: (min(b, planes - 1 - b), -b)):
            if kind == ENCODER:

                @pl.when(owner & (d != b))
                def _():
                    received(buffer.at[b, rank], z_recv.at[b])

            else:
                finish_rows(b)
            for shift in range(1, tensors):
                send(owner, buffer.at[b, rank], buffer.at[b, rank], e_send.at[kind, b, shift],
                     e_recv.at[kind, b, rank], tensor=lax.rem(t + shift, tensors))

    def have_spread(kind, buffer, b):
        for k in range(sections):

            @pl.when(k * groups + d // blocks != t)
            def _():
                received(buffer.at[b, k], e_recv.at[kind, b, k])

    def forward_rows():
        for order, held, sem, has, to in (
            (reversed(range(blocks)), rs_up, r_up, d > 0, 1),
            (range(blocks), rs_dn, r_dn, d < planes - 1, planes - 1),
        ):
            for i in order:
                plane = group * blocks + i
                moving = has & ((plane > d) if to == 1 else (plane < d))
                for b in range(planes):

                    @pl.when(moving)
                    def _():
                        received(held.at[i, b], sem.at[i, b])
                        rs_out[i, b] = picks[b, :, pl.ds(i * depth, depth)] + held[i, b]

                    send(moving, rs_out.at[i, b], held.at[i, b], r_send.at[i, b], sem.at[i, b],
                         dp=lax.rem(d + to, planes))

    def finish_rows(b):
        for i in range(blocks):
            mine = group * blocks + i == d

            @pl.when(mine)
            def _():
                x_dec[b, rank] = picks[b, :, pl.ds(i * depth, depth)]

            for has, held, sem in ((d > 0, rs_up, r_up), (d < planes - 1, rs_dn, r_dn)):

                @pl.when(mine & has)
                def _():
                    received(held.at[i, b], sem.at[i, b])
                    x_dec[b, rank] = x_dec[b, rank] + held[i, b]

    def product(j, x, b, n):
        cols = pl.ds(pl.multiple_of(n * HD, HD), HD)
        total = None
        for k in range(sections):
            term = jnp.dot(x[b, k], wbuf[j, k, :, cols], preferred_element_type=jnp.float32)
            total = term if total is None else total + term
        return total

    def chain(j, x, gate):
        for step in range(planes - 1):
            for b, to, held, sem, has in (
                (planes - 1 - step, 1, up, c_up, d > 0),
                (step, planes - 1, dn, c_dn, d < planes - 1),
            ):

                @pl.when(gate & (b > d if to == 1 else b < d))
                def _():
                    @pl.loop(0, chunks)
                    def _(n):
                        @pl.when(has)
                        def _():
                            received(held.at[j, b, n], sem.at[j, b, n])

                        total = product(j, x, b, n) + held[j, b, n].astype(jnp.float32)
                        sums[j, b, n] = total.astype(jnp.bfloat16)
                        remote(sums.at[j, b, n], held.at[j, b, n], c_send.at[j, b, n], sem.at[j, b, n],
                               dp=lax.rem(d + to, planes)).start()

    def whole(j, x, n):
        total = product(j, x, d, n)

        @pl.when(d > 0)
        def _():
            received(up.at[j, d, n], c_up.at[j, d, n])

        @pl.when(d < planes - 1)
        def _():
            received(dn.at[j, d, n], c_dn.at[j, d, n])

        rest = up[j, d, n].astype(jnp.float32) + dn[j, d, n].astype(jnp.float32)
        return (total + rest).astype(jnp.bfloat16)

    def finish(j, x, result):
        @pl.loop(0, chunks)
        def _(n):
            result[:, pl.ds(pl.multiple_of(n * HD, HD), HD)] = whole(j, x, n)

    def attend():
        @pl.loop(0, chunks)
        def _(head):
            cols = pl.ds(pl.multiple_of(head * HD, HD), HD)
            queries = whole(QUERY, x_dec, head)
            scores = [
                lax.dot_general(queries, k_all[k, :, cols], (((1,), (1,)), ((), ())),
                                preferred_element_type=jnp.float32) * HD ** (-0.5)
                for k in range(sections)
            ]
            peak = functools.reduce(jnp.maximum, [jnp.max(a, axis=-1, keepdims=True) for a in scores])
            weights = [jnp.exp(a - peak) for a in scores]
            weight_sum = sum(jnp.sum(a, axis=-1, keepdims=True) for a in weights)
            total = sum(
                jnp.dot(a.astype(jnp.bfloat16), v_all[k, :, cols], preferred_element_type=jnp.float32)
                for k, a in enumerate(weights)
            )
            out[:, cols] = (total / weight_sum).astype(jnp.bfloat16)

    def share(j, result):
        for shift in range(1, sections):
            send(always, result.at[s], result.at[s], o_send.at[j, shift], o_recv.at[j, s],
                 section=lax.rem(s + shift, sections))

    spread(ENCODER, x_enc)
    start_weight(VALUE, w_value)
    forward_rows()

    def keys(gate):
        @pl.when(gate)
        def _():
            for b in range(planes):
                have_spread(ENCODER, x_enc, b)
            have_weight(KEY)
            local[KEY].wait()

        chain(KEY, x_enc, gate)

    keys(edge)
    spread(DECODER, x_dec)
    keys(jnp.logical_not(edge))
    local[VALUE].wait()
    local[QUERY].wait()
    have_weight(VALUE)
    start_weight(QUERY, w_query)
    chain(VALUE, x_enc, always)
    finish(KEY, x_enc, k_all.at[s])
    share(KEY, k_all)
    for b in range(planes):
        have_spread(DECODER, x_dec, b)
    have_weight(QUERY)
    chain(QUERY, x_dec, always)
    finish(VALUE, x_enc, v_all.at[s])
    share(VALUE, v_all)
    for j, result in ((KEY, k_all), (VALUE, v_all)):
        for shift in range(1, sections):
            other = lax.rem(s + shift, sections)
            received(result.at[other], o_recv.at[j, other])
    attend()
    for when, copy in sent:
        pl.when(when)(copy.wait_send)
    for j in range(3):
        for b in range(planes):

            @pl.when(b != d)
            def _():
                @pl.loop(0, chunks)
                def _(n):
                    remote(sums.at[j, b, n], sums.at[j, b, n], c_send.at[j, b, n], c_up.at[j, b, n],
                           dp=lax.rem(d + 1, planes)).wait_send()


def projections(mesh, enc, picks, w_key, w_value, w_query):
    sections, tensors, planes = (mesh.shape[a] for a in ("section", "tensor", "dp"))
    positions = enc.shape[0]
    depth, columns = w_key.shape
    blocks = enc.shape[1] // depth
    bf16 = jnp.bfloat16
    dma = pltpu.SemaphoreType.DMA
    rows = (planes, sections, positions, depth)
    moving = (blocks, planes, positions, depth)
    chains = (3, planes, columns // HD, positions, HD)
    vmem = pl.BlockSpec(memory_space=pltpu.VMEM)
    hbm = pl.BlockSpec(memory_space=pl.ANY)
    return pl.pallas_call(
        functools.partial(project_kernel, sections, tensors, planes),
        out_shape=jax.ShapeDtypeStruct((positions, columns), bf16),
        in_specs=[vmem, vmem, hbm, hbm, hbm],
        out_specs=vmem,
        scratch_shapes=[
            pltpu.VMEM((sections, positions, columns), bf16),
            pltpu.VMEM((sections, positions, columns), bf16),
            pltpu.VMEM((3, sections, depth, columns), bf16),
            pltpu.VMEM(rows, bf16),
            pltpu.VMEM(rows, bf16),
            pltpu.VMEM(moving, bf16),
            pltpu.VMEM(moving, bf16),
            pltpu.VMEM(moving, bf16),
            pltpu.VMEM(chains, bf16),
            pltpu.VMEM(chains, bf16),
            pltpu.VMEM(chains, bf16),
            dma((3,)),
            dma((3, sections)),
            dma((3, sections)),
            dma((blocks,)),
            dma((planes,)),
            dma((2, planes, tensors)),
            dma((2, planes, sections)),
            dma((blocks, planes)),
            dma((blocks, planes)),
            dma((blocks, planes)),
            dma(chains[:3]),
            dma(chains[:3]),
            dma(chains[:3]),
            dma((2, sections)),
            dma((2, sections)),
        ],
        compiler_params=pltpu.CompilerParams(
            collective_id=0, has_side_effects=True, vmem_limit_bytes=56 * 2**20
        ),
        cost_estimate=pl.CostEstimate(
            flops=6 * planes * positions * sections * depth * columns,
            bytes_accessed=2 * (picks.size + 3 * w_key.size),
            transcendentals=0,
        ),
    )(enc, picks, w_key, w_value, w_query)


def make(mesh):
    def on_device(target_ids, embed_table, encoder_out, w_query, w_key, w_value):
        table_rows = embed_table.shape[0]
        offset_ids = target_ids - lax.axis_index("dp") * table_rows
        inside = (offset_ids >= 0) & (offset_ids < table_rows)
        picked = jnp.take(
            embed_table, jnp.where(inside, offset_ids, table_rows), axis=0, mode="fill", fill_value=0
        )
        return projections(mesh, encoder_out[0], picked, w_key, w_value, w_query)[None]

    return on_device


def solution(mesh):
    in_specs = (
        P(None, "section"),
        P("dp", "tensor"),
        P("dp", "section", "tensor"),
        P(("section", "dp"), "tensor"),
        P(("section", "dp"), "tensor"),
        P(("section", "dp"), "tensor"),
    )
    out_specs = P("dp", "section", "tensor")
    return jax.shard_map(
        make(mesh), mesh=mesh, in_specs=in_specs, out_specs=out_specs, check_vma=False
    )
```

```python
import functools

import jax
import jax.numpy as jnp
from jax import lax
from jax.experimental import pallas as pl
from jax.experimental.pallas import tpu as pltpu
from jax.sharding import PartitionSpec as P

HD = 256
KEY, VALUE, QUERY = 0, 1, 2
ENCODER, DECODER = 0, 1


def project_kernel(
    sections, tensors, planes,
    enc, picks, w_key, w_value, w_query,
    out,
    k_all, v_all, wbuf, x_enc, x_dec, rs_up, rs_dn, rs_out, sums, held_sums,
    w_local, w_send, w_recv, z_send, z_recv, e_send, e_recv,
    r_send, r_up, r_dn, c_send, c_recv, o_send, o_recv,
):
    s, t, d = lax.axis_index("section"), lax.axis_index("tensor"), lax.axis_index("dp")
    depth, columns = w_key.shape
    blocks = enc.shape[1] // depth
    groups = planes // blocks
    rank, group = t // groups, lax.rem(t, groups)
    owner = group == d // blocks
    chunks = columns // HD
    edge = (d == 0) | (d == planes - 1)
    sent = []

    def remote(src, dst, send_sem, recv_sem, **device):
        return pltpu.make_async_remote_copy(
            src_ref=src, dst_ref=dst, send_sem=send_sem, recv_sem=recv_sem,
            device_id=device, device_id_type=pl.DeviceIdType.MESH,
        )

    def send(when, src, dst, send_sem, recv_sem, **device):
        copy = remote(src, dst, send_sem, recv_sem, **device)
        sent.append((when, copy))

        @pl.when(when)
        def _():
            copy.start()

    def received(dst, recv_sem):
        remote(dst, dst, c_send.at[0, 0, 0], recv_sem, dp=lax.rem(d + 1, planes)).wait_recv()

    always = d >= 0
    barrier = pltpu.get_barrier_semaphore()
    for axis, index, size in (("section", s, sections), ("tensor", t, tensors), ("dp", d, planes)):
        for shift in range(1, size):
            pl.semaphore_signal(
                barrier, inc=1, device_id={axis: lax.rem(index + shift, size)},
                device_id_type=pl.DeviceIdType.MESH,
            )
    pl.semaphore_wait(barrier, sections + tensors + planes - 3)

    def start_weight(j, weight):
        for shift in range(1, sections):
            send(always, weight, wbuf.at[j, s], w_send.at[j, shift], w_recv.at[j, s],
                 section=lax.rem(s + shift, sections))

    def have_weight(j):
        for shift in range(1, sections):
            other = lax.rem(s + shift, sections)
            received(wbuf.at[j, other], w_recv.at[j, other])

    def part(ref, i):
        return ref.at[:, pl.ds(i * depth, depth)]

    for i in range(blocks):
        plane = group * blocks + i
        send(plane != d, part(enc, i), x_enc.at[d, rank], z_send.at[i], z_recv.at[d], dp=plane)
    start_weight(KEY, w_key)
    for order, held, sem, end, to in (
        (reversed(range(blocks)), rs_up, r_up, 0, 1),
        (range(blocks), rs_dn, r_dn, planes - 1, planes - 1),
    ):
        for i in order:
            plane = group * blocks + i
            moving = (d == end) & ((plane > d) if to == 1 else (plane < d))
            for b in range(planes):
                src = picks.at[b, :, pl.ds(i * depth, depth)]
                send(moving, src, held.at[i, b], r_send.at[i, b], sem.at[i, b], dp=lax.rem(d + to, planes))
    local = [
        pltpu.make_async_copy(w, wbuf.at[j, s], w_local.at[j])
        for j, w in enumerate((w_key, w_value, w_query))
    ]
    for copy in local:
        copy.start()
    for i in range(blocks):

        @pl.when(group * blocks + i == d)
        def _():
            x_enc[d, rank] = enc[:, pl.ds(i * depth, depth)]

    def clear(way):
        @pl.loop(0, 3 * chunks)
        def _(n):
            held_sums[way, n // chunks, d, lax.rem(n, chunks)] = jnp.zeros((enc.shape[0], HD), enc.dtype)

    pl.when(d == 0)(lambda: clear(0))
    pl.when(d == planes - 1)(lambda: clear(1))

    def spread(kind, buffer):
        for b in sorted(range(planes), key=lambda b: (min(b, planes - 1 - b), -b)):
            if kind == ENCODER:

                @pl.when(owner & (d != b))
                def _():
                    received(buffer.at[b, rank], z_recv.at[b])

            else:
                finish_rows(b)
            for shift in range(1, tensors):
                send(owner, buffer.at[b, rank], buffer.at[b, rank], e_send.at[kind, b, shift],
                     e_recv.at[kind, b, rank], tensor=lax.rem(t + shift, tensors))

    def have_spread(kind, buffer, b):
        for k in range(sections):

            @pl.when(k * groups + d // blocks != t)
            def _():
                received(buffer.at[b, k], e_recv.at[kind, b, k])

    def forward_rows():
        for order, held, sem, has, to in (
            (reversed(range(blocks)), rs_up, r_up, d > 0, 1),
            (range(blocks), rs_dn, r_dn, d < planes - 1, planes - 1),
        ):
            for i in order:
                plane = group * blocks + i
                moving = has & ((plane > d) if to == 1 else (plane < d))
                for b in range(planes):

                    @pl.when(moving)
                    def _():
                        received(held.at[i, b], sem.at[i, b])
                        rs_out[i, b] = picks[b, :, pl.ds(i * depth, depth)] + held[i, b]

                    send(moving, rs_out.at[i, b], held.at[i, b], r_send.at[i, b], sem.at[i, b],
                         dp=lax.rem(d + to, planes))

    def finish_rows(b):
        for i in range(blocks):
            mine = group * blocks + i == d

            @pl.when(mine)
            def _():
                x_dec[b, rank] = picks[b, :, pl.ds(i * depth, depth)]

            for has, held, sem in ((d > 0, rs_up, r_up), (d < planes - 1, rs_dn, r_dn)):

                @pl.when(mine & has)
                def _():
                    received(held.at[i, b], sem.at[i, b])
                    x_dec[b, rank] = x_dec[b, rank] + held[i, b]

    def product(j, x, b, n):
        cols = pl.ds(pl.multiple_of(n * HD, HD), HD)
        total = None
        for k in range(sections):
            term = jnp.dot(x[b, k], wbuf[j, k, :, cols], preferred_element_type=jnp.float32)
            total = term if total is None else total + term
        return total

    def chain(j, x, gate):
        near = jnp.where(d < planes // 2, 0, 1)
        for step in range(planes - 1):
            for way in (near, 1 - near):
                rising = way == 0
                b = jnp.where(rising, planes - 1 - step, step)
                has = jnp.where(rising, d, planes - 1 - d) > 0
                to = lax.rem(d + jnp.where(rising, 1, planes - 1), planes)

                @pl.when(gate & (jnp.where(rising, b - d, d - b) > 0))
                def _():
                    @pl.loop(0, chunks)
                    def _(n):
                        total = product(j, x, b, n)

                        @pl.when(has)
                        def _():
                            received(held_sums.at[way, j, b, n], c_recv.at[way, j, b, n])
                            rest = held_sums[way, j, b, n].astype(jnp.float32)
                            sums[j, b, n] = (total + rest).astype(jnp.bfloat16)

                        @pl.when(jnp.logical_not(has))
                        def _():
                            sums[j, b, n] = total.astype(jnp.bfloat16)

                        remote(sums.at[j, b, n], held_sums.at[way, j, b, n], c_send.at[j, b, n],
                               c_recv.at[way, j, b, n], dp=to).start()

    def whole(j, x, n):
        total = product(j, x, d, n)
        for way, has in ((0, d > 0), (1, d < planes - 1)):

            @pl.when(has)
            def _():
                received(held_sums.at[way, j, d, n], c_recv.at[way, j, d, n])

        rest = held_sums[0, j, d, n].astype(jnp.float32) + held_sums[1, j, d, n].astype(jnp.float32)
        return (total + rest).astype(jnp.bfloat16)

    def finish(j, x, result):
        @pl.loop(0, chunks)
        def _(n):
            result[:, pl.ds(pl.multiple_of(n * HD, HD), HD)] = whole(j, x, n)

    def attend():
        @pl.loop(0, chunks)
        def _(head):
            cols = pl.ds(pl.multiple_of(head * HD, HD), HD)
            queries = whole(QUERY, x_dec, head)
            scores = [
                lax.dot_general(queries, k_all[k, :, cols], (((1,), (1,)), ((), ())),
                                preferred_element_type=jnp.float32) * HD ** (-0.5)
                for k in range(sections)
            ]
            peak = functools.reduce(jnp.maximum, [jnp.max(a, axis=-1, keepdims=True) for a in scores])
            weights = [jnp.exp(a - peak) for a in scores]
            weight_sum = sum(jnp.sum(a, axis=-1, keepdims=True) for a in weights)
            total = sum(
                jnp.dot(a.astype(jnp.bfloat16), v_all[k, :, cols], preferred_element_type=jnp.float32)
                for k, a in enumerate(weights)
            )
            out[:, cols] = (total / weight_sum).astype(jnp.bfloat16)

    def share(j, result, gate):
        for shift in range(1, sections):
            send(gate, result.at[s], result.at[s], o_send.at[j, shift], o_recv.at[j, s],
                 section=lax.rem(s + shift, sections))

    spread(ENCODER, x_enc)
    start_weight(VALUE, w_value)
    forward_rows()

    def keys(gate):
        @pl.when(gate)
        def _():
            for b in range(planes):
                have_spread(ENCODER, x_enc, b)
            have_weight(KEY)
            local[KEY].wait()

        chain(KEY, x_enc, gate)

    keys(edge)
    spread(DECODER, x_dec)
    keys(jnp.logical_not(edge))
    local[VALUE].wait()
    local[QUERY].wait()
    have_weight(VALUE)
    start_weight(QUERY, w_query)
    chain(VALUE, x_enc, always)

    def keys_done(gate):
        @pl.when(gate)
        def _():
            finish(KEY, x_enc, k_all.at[s])

        share(KEY, k_all, gate)

    keys_done(jnp.logical_not(edge))
    for b in range(planes):
        have_spread(DECODER, x_dec, b)
    have_weight(QUERY)
    chain(QUERY, x_dec, always)
    keys_done(edge)
    finish(VALUE, x_enc, v_all.at[s])
    share(VALUE, v_all, always)
    for j, result in ((KEY, k_all), (VALUE, v_all)):
        for shift in range(1, sections):
            other = lax.rem(s + shift, sections)
            received(result.at[other], o_recv.at[j, other])
    attend()
    for when, copy in sent:
        pl.when(when)(copy.wait_send)
    for j in range(3):
        for b in range(planes):

            @pl.when(b != d)
            def _():
                @pl.loop(0, chunks)
                def _(n):
                    remote(sums.at[j, b, n], sums.at[j, b, n], c_send.at[j, b, n], c_recv.at[0, j, b, n],
                           dp=lax.rem(d + 1, planes)).wait_send()


def projections(mesh, enc, picks, w_key, w_value, w_query):
    sections, tensors, planes = (mesh.shape[a] for a in ("section", "tensor", "dp"))
    positions = enc.shape[0]
    depth, columns = w_key.shape
    blocks = enc.shape[1] // depth
    bf16 = jnp.bfloat16
    dma = pltpu.SemaphoreType.DMA
    rows = (planes, sections, positions, depth)
    moving = (blocks, planes, positions, depth)
    chains = (3, planes, columns // HD, positions, HD)
    vmem = pl.BlockSpec(memory_space=pltpu.VMEM)
    hbm = pl.BlockSpec(memory_space=pl.ANY)
    return pl.pallas_call(
        functools.partial(project_kernel, sections, tensors, planes),
        out_shape=jax.ShapeDtypeStruct((positions, columns), bf16),
        in_specs=[vmem, vmem, hbm, hbm, hbm],
        out_specs=vmem,
        scratch_shapes=[
            pltpu.VMEM((sections, positions, columns), bf16),
            pltpu.VMEM((sections, positions, columns), bf16),
            pltpu.VMEM((3, sections, depth, columns), bf16),
            pltpu.VMEM(rows, bf16),
            pltpu.VMEM(rows, bf16),
            pltpu.VMEM(moving, bf16),
            pltpu.VMEM(moving, bf16),
            pltpu.VMEM(moving, bf16),
            pltpu.VMEM(chains, bf16),
            pltpu.VMEM((2,) + chains, bf16),
            dma((3,)),
            dma((3, sections)),
            dma((3, sections)),
            dma((blocks,)),
            dma((planes,)),
            dma((2, planes, tensors)),
            dma((2, planes, sections)),
            dma((blocks, planes)),
            dma((blocks, planes)),
            dma((blocks, planes)),
            dma(chains[:3]),
            dma((2,) + chains[:3]),
            dma((2, sections)),
            dma((2, sections)),
        ],
        compiler_params=pltpu.CompilerParams(
            collective_id=0, has_side_effects=True, vmem_limit_bytes=56 * 2**20
        ),
        cost_estimate=pl.CostEstimate(
            flops=6 * planes * positions * sections * depth * columns,
            bytes_accessed=2 * (picks.size + 3 * w_key.size),
            transcendentals=0,
        ),
    )(enc, picks, w_key, w_value, w_query)


def make(mesh):
    def on_device(target_ids, embed_table, encoder_out, w_query, w_key, w_value):
        table_rows = embed_table.shape[0]
        offset_ids = target_ids - lax.axis_index("dp") * table_rows
        inside = (offset_ids >= 0) & (offset_ids < table_rows)
        picked = jnp.take(
            embed_table, jnp.where(inside, offset_ids, table_rows), axis=0, mode="fill", fill_value=0
        )
        return projections(mesh, encoder_out[0], picked, w_key, w_value, w_query)[None]

    return on_device


def solution(mesh):
    in_specs = (
        P(None, "section"),
        P("dp", "tensor"),
        P("dp", "section", "tensor"),
        P(("section", "dp"), "tensor"),
        P(("section", "dp"), "tensor"),
        P(("section", "dp"), "tensor"),
    )
    out_specs = P("dp", "section", "tensor")
    return jax.shard_map(
        make(mesh), mesh=mesh, in_specs=in_specs, out_specs=out_specs, check_vma=False
    )
```

```python
import functools

import jax
import jax.numpy as jnp
from jax import lax
from jax.experimental import pallas as pl
from jax.experimental.pallas import tpu as pltpu
from jax.sharding import PartitionSpec as P

HD = 256
KEY, VALUE, QUERY = 0, 1, 2
ENCODER, DECODER = 0, 1


def project_kernel(
    sections, tensors, planes,
    enc, picks, w_key, w_value, w_query,
    out,
    k_all, v_all, wbuf, x_enc, x_dec, rs_up, rs_dn, rs_out, sums, held_sums,
    w_local, w_send, w_recv, z_send, z_recv, e_send, e_recv,
    r_send, r_up, r_dn, c_send, c_recv, o_send, o_recv,
):
    s, t, d = lax.axis_index("section"), lax.axis_index("tensor"), lax.axis_index("dp")
    depth, columns = w_key.shape
    blocks = enc.shape[1] // depth
    groups = planes // blocks
    rank, group = t // groups, lax.rem(t, groups)
    owner = group == d // blocks
    chunks = columns // HD
    edge = (d == 0) | (d == planes - 1)
    sent = []

    def remote(src, dst, send_sem, recv_sem, **device):
        return pltpu.make_async_remote_copy(
            src_ref=src, dst_ref=dst, send_sem=send_sem, recv_sem=recv_sem,
            device_id=device, device_id_type=pl.DeviceIdType.MESH,
        )

    def send(when, src, dst, send_sem, recv_sem, **device):
        copy = remote(src, dst, send_sem, recv_sem, **device)
        sent.append((when, copy))

        @pl.when(when)
        def _():
            copy.start()

    def received(dst, recv_sem):
        remote(dst, dst, c_send.at[0, 0, 0], recv_sem, dp=lax.rem(d + 1, planes)).wait_recv()

    always = d >= 0
    barrier = pltpu.get_barrier_semaphore()
    for axis, index, size in (("section", s, sections), ("tensor", t, tensors), ("dp", d, planes)):
        for shift in range(1, size):
            pl.semaphore_signal(
                barrier, inc=1, device_id={axis: lax.rem(index + shift, size)},
                device_id_type=pl.DeviceIdType.MESH,
            )
    pl.semaphore_wait(barrier, sections + tensors + planes - 3)

    def start_weight(j, weight):
        for shift in range(1, sections):
            send(always, weight, wbuf.at[j, s], w_send.at[j, shift], w_recv.at[j, s],
                 section=lax.rem(s + shift, sections))

    def have_weight(j):
        for shift in range(1, sections):
            other = lax.rem(s + shift, sections)
            received(wbuf.at[j, other], w_recv.at[j, other])

    def part(ref, i):
        return ref.at[:, pl.ds(i * depth, depth)]

    for i in range(blocks):
        plane = group * blocks + i
        send(plane != d, part(enc, i), x_enc.at[d, rank], z_send.at[i], z_recv.at[d], dp=plane)
    start_weight(KEY, w_key)
    for order, held, sem, end, to in (
        (reversed(range(blocks)), rs_up, r_up, 0, 1),
        (range(blocks), rs_dn, r_dn, planes - 1, planes - 1),
    ):
        for i in order:
            plane = group * blocks + i
            moving = (d == end) & ((plane > d) if to == 1 else (plane < d))
            for b in range(planes):
                src = picks.at[b, :, pl.ds(i * depth, depth)]
                send(moving, src, held.at[i, b], r_send.at[i, b], sem.at[i, b], dp=lax.rem(d + to, planes))
    local = [
        pltpu.make_async_copy(w, wbuf.at[j, s], w_local.at[j])
        for j, w in enumerate((w_key, w_value, w_query))
    ]
    for copy in local:
        copy.start()
    for i in range(blocks):

        @pl.when(group * blocks + i == d)
        def _():
            x_enc[d, rank] = enc[:, pl.ds(i * depth, depth)]

    def clear(way):
        @pl.loop(0, 3 * chunks)
        def _(n):
            held_sums[way, n // chunks, d, lax.rem(n, chunks)] = jnp.zeros((enc.shape[0], HD), enc.dtype)

    pl.when(d == 0)(lambda: clear(0))
    pl.when(d == planes - 1)(lambda: clear(1))

    def spread(kind, buffer):
        for b in sorted(range(planes), key=lambda b: (min(b, planes - 1 - b), -b)):
            if kind == ENCODER:

                @pl.when(owner & (d != b))
                def _():
                    received(buffer.at[b, rank], z_recv.at[b])

            else:
                finish_rows(b)
            for shift in range(1, tensors):
                send(owner, buffer.at[b, rank], buffer.at[b, rank], e_send.at[kind, b, shift],
                     e_recv.at[kind, b, rank], tensor=lax.rem(t + shift, tensors))

    def have_spread(kind, buffer, b):
        for k in range(sections):

            @pl.when(k * groups + d // blocks != t)
            def _():
                received(buffer.at[b, k], e_recv.at[kind, b, k])

    def forward_rows():
        for order, held, sem, has, to in (
            (reversed(range(blocks)), rs_up, r_up, d > 0, 1),
            (range(blocks), rs_dn, r_dn, d < planes - 1, planes - 1),
        ):
            for i in order:
                plane = group * blocks + i
                moving = has & ((plane > d) if to == 1 else (plane < d))
                for b in range(planes):

                    @pl.when(moving)
                    def _():
                        received(held.at[i, b], sem.at[i, b])
                        rs_out[i, b] = picks[b, :, pl.ds(i * depth, depth)] + held[i, b]

                    send(moving, rs_out.at[i, b], held.at[i, b], r_send.at[i, b], sem.at[i, b],
                         dp=lax.rem(d + to, planes))

    def finish_rows(b):
        for i in range(blocks):
            mine = group * blocks + i == d

            @pl.when(mine)
            def _():
                x_dec[b, rank] = picks[b, :, pl.ds(i * depth, depth)]

            for has, held, sem in ((d > 0, rs_up, r_up), (d < planes - 1, rs_dn, r_dn)):

                @pl.when(mine & has)
                def _():
                    received(held.at[i, b], sem.at[i, b])
                    x_dec[b, rank] = x_dec[b, rank] + held[i, b]

    def product(j, x, b, n):
        cols = pl.ds(pl.multiple_of(n * HD, HD), HD)
        total = None
        for k in range(sections):
            term = jnp.dot(x[b, k], wbuf[j, k, :, cols], preferred_element_type=jnp.float32)
            total = term if total is None else total + term
        return total

    def chain(j, x, gate):
        near = jnp.where(d < planes // 2, 0, 1)
        for step in range(planes - 1):
            for way in (near, 1 - near):
                rising = way == 0
                b = jnp.where(rising, planes - 1 - step, step)
                has = jnp.where(rising, d, planes - 1 - d) > 0
                to = lax.rem(d + jnp.where(rising, 1, planes - 1), planes)

                @pl.when(gate & (jnp.where(rising, b - d, d - b) > 0))
                def _():
                    @pl.loop(0, chunks)
                    def _(n):
                        total = product(j, x, b, n)

                        @pl.when(has)
                        def _():
                            received(held_sums.at[way, j, b, n], c_recv.at[way, j, b, n])
                            rest = held_sums[way, j, b, n].astype(jnp.float32)
                            sums[j, b, n] = (total + rest).astype(jnp.bfloat16)

                        @pl.when(jnp.logical_not(has))
                        def _():
                            sums[j, b, n] = total.astype(jnp.bfloat16)

                        remote(sums.at[j, b, n], held_sums.at[way, j, b, n], c_send.at[j, b, n],
                               c_recv.at[way, j, b, n], dp=to).start()

    def whole(j, x, n):
        total = product(j, x, d, n)
        for way, has in ((0, d > 0), (1, d < planes - 1)):

            @pl.when(has)
            def _():
                received(held_sums.at[way, j, d, n], c_recv.at[way, j, d, n])

        rest = held_sums[0, j, d, n].astype(jnp.float32) + held_sums[1, j, d, n].astype(jnp.float32)
        return (total + rest).astype(jnp.bfloat16)

    def finish(j, x, result):
        @pl.loop(0, chunks)
        def _(n):
            result[:, pl.ds(pl.multiple_of(n * HD, HD), HD)] = whole(j, x, n)

    def attend():
        @pl.loop(0, chunks)
        def _(head):
            cols = pl.ds(pl.multiple_of(head * HD, HD), HD)
            queries = whole(QUERY, x_dec, head)
            scores = [
                lax.dot_general(queries, k_all[k, :, cols], (((1,), (1,)), ((), ())),
                                preferred_element_type=jnp.float32) * HD ** (-0.5)
                for k in range(sections)
            ]
            peak = functools.reduce(jnp.maximum, [jnp.max(a, axis=-1, keepdims=True) for a in scores])
            weights = [jnp.exp(a - peak) for a in scores]
            weight_sum = sum(jnp.sum(a, axis=-1, keepdims=True) for a in weights)
            total = sum(
                jnp.dot(a.astype(jnp.bfloat16), v_all[k, :, cols], preferred_element_type=jnp.float32)
                for k, a in enumerate(weights)
            )
            out[:, cols] = (total / weight_sum).astype(jnp.bfloat16)

    def share(j, result, gate):
        for shift in range(1, sections):
            send(gate, result.at[s], result.at[s], o_send.at[j, shift], o_recv.at[j, s],
                 section=lax.rem(s + shift, sections))

    spread(ENCODER, x_enc)
    start_weight(VALUE, w_value)
    forward_rows()

    def keys(gate):
        @pl.when(gate)
        def _():
            for b in range(planes):
                have_spread(ENCODER, x_enc, b)
            have_weight(KEY)
            local[KEY].wait()

        chain(KEY, x_enc, gate)

    keys(edge)
    spread(DECODER, x_dec)
    keys(jnp.logical_not(edge))
    local[VALUE].wait()
    local[QUERY].wait()
    have_weight(VALUE)
    start_weight(QUERY, w_query)
    chain(VALUE, x_enc, always)

    def memory_done(gate):
        for j, result in ((KEY, k_all), (VALUE, v_all)):

            @pl.when(gate)
            def _():
                finish(j, x_enc, result.at[s])

            share(j, result, gate)

    memory_done(jnp.logical_not(edge))
    for b in range(planes):
        have_spread(DECODER, x_dec, b)
    have_weight(QUERY)
    chain(QUERY, x_dec, always)
    memory_done(edge)
    for j, result in ((KEY, k_all), (VALUE, v_all)):
        for shift in range(1, sections):
            other = lax.rem(s + shift, sections)
            received(result.at[other], o_recv.at[j, other])
    attend()
    for when, copy in sent:
        pl.when(when)(copy.wait_send)
    for j in range(3):
        for b in range(planes):

            @pl.when(b != d)
            def _():
                @pl.loop(0, chunks)
                def _(n):
                    remote(sums.at[j, b, n], sums.at[j, b, n], c_send.at[j, b, n], c_recv.at[0, j, b, n],
                           dp=lax.rem(d + 1, planes)).wait_send()


def projections(mesh, enc, picks, w_key, w_value, w_query):
    sections, tensors, planes = (mesh.shape[a] for a in ("section", "tensor", "dp"))
    positions = enc.shape[0]
    depth, columns = w_key.shape
    blocks = enc.shape[1] // depth
    bf16 = jnp.bfloat16
    dma = pltpu.SemaphoreType.DMA
    rows = (planes, sections, positions, depth)
    moving = (blocks, planes, positions, depth)
    chains = (3, planes, columns // HD, positions, HD)
    vmem = pl.BlockSpec(memory_space=pltpu.VMEM)
    hbm = pl.BlockSpec(memory_space=pl.ANY)
    return pl.pallas_call(
        functools.partial(project_kernel, sections, tensors, planes),
        out_shape=jax.ShapeDtypeStruct((positions, columns), bf16),
        in_specs=[vmem, vmem, hbm, hbm, hbm],
        out_specs=vmem,
        scratch_shapes=[
            pltpu.VMEM((sections, positions, columns), bf16),
            pltpu.VMEM((sections, positions, columns), bf16),
            pltpu.VMEM((3, sections, depth, columns), bf16),
            pltpu.VMEM(rows, bf16),
            pltpu.VMEM(rows, bf16),
            pltpu.VMEM(moving, bf16),
            pltpu.VMEM(moving, bf16),
            pltpu.VMEM(moving, bf16),
            pltpu.VMEM(chains, bf16),
            pltpu.VMEM((2,) + chains, bf16),
            dma((3,)),
            dma((3, sections)),
            dma((3, sections)),
            dma((blocks,)),
            dma((planes,)),
            dma((2, planes, tensors)),
            dma((2, planes, sections)),
            dma((blocks, planes)),
            dma((blocks, planes)),
            dma((blocks, planes)),
            dma(chains[:3]),
            dma((2,) + chains[:3]),
            dma((2, sections)),
            dma((2, sections)),
        ],
        compiler_params=pltpu.CompilerParams(
            collective_id=0, has_side_effects=True, vmem_limit_bytes=56 * 2**20
        ),
        cost_estimate=pl.CostEstimate(
            flops=6 * planes * positions * sections * depth * columns,
            bytes_accessed=2 * (picks.size + 3 * w_key.size),
            transcendentals=0,
        ),
    )(enc, picks, w_key, w_value, w_query)


def make(mesh):
    def on_device(target_ids, embed_table, encoder_out, w_query, w_key, w_value):
        table_rows = embed_table.shape[0]
        offset_ids = target_ids - lax.axis_index("dp") * table_rows
        inside = (offset_ids >= 0) & (offset_ids < table_rows)
        picked = jnp.take(
            embed_table, jnp.where(inside, offset_ids, table_rows), axis=0, mode="fill", fill_value=0
        )
        return projections(mesh, encoder_out[0], picked, w_key, w_value, w_query)[None]

    return on_device


def solution(mesh):
    in_specs = (
        P(None, "section"),
        P("dp", "tensor"),
        P("dp", "section", "tensor"),
        P(("section", "dp"), "tensor"),
        P(("section", "dp"), "tensor"),
        P(("section", "dp"), "tensor"),
    )
    out_specs = P("dp", "section", "tensor")
    return jax.shard_map(
        make(mesh), mesh=mesh, in_specs=in_specs, out_specs=out_specs, check_vma=False
    )
```
